128 devices in a mesh: row: 8 (over x, core), col: 16 (over z, y).
Axes of the slice: x: 4, y: 4, z: 4, core: 2. Of those that a mesh axis runs over, the one named last changes fastest.
Arguments:
- leaf_up: bfloat16 [65536, 3, 128], P(('row', 'col')), may hold values from -6 to 6
- child_to_parent: bfloat16 [8, 128, 128], replicated, may hold values from -0.1875 to 0.1875
- translations: bfloat16 [316, 128, 128], replicated, may hold values from -0.0390625 to 0.0390625
- parent_to_child: bfloat16 [8, 128, 128], replicated, may hold values from -0.5 to 0.5
- check_to_density: bfloat16 [128, 128], replicated, may hold values from -0.375 to 0.375
- leaf_lists: int32 [65536, 316], P(('row', 'col')), may hold values from -1 to 4607, as said below
- leaf_ghosts: int32 [128, 16, 256], P(('row', 'col')), may hold values from 0 to 511, as said below
- parent_lists: int32 [8192, 316], P(('row', 'col')), may hold values from -1 to 575, as said below
- parent_ghosts: int32 [128, 16, 32], P(('row', 'col')), may hold values from 0 to 63, as said below
Outputs:
- leaf_down: bfloat16 [65536, 3, 128], P(('row', 'col'))
The draws below stay inside these ranges and needn't reach their ends.
Inputs may be any that keep to these rules, and one draw needn't show every extreme that they name: `leaf_lists`: positions name a local box or a ghost slot as in the reference program; a ghost slot's sender e = d - o(j) is always a device of the slice; about a fifth to three fifths of a leaf's entries are present, the share set per device. The 256 entries of leaf_ghosts[e, j, :] are distinct. `parent_lists`: sources of a parent lie in its own row of devices. The 32 entries of parent_ghosts[e, c, :] are distinct.
All inputs are finite; a program needn't handle non-finite values.
Results may differ from the reference program's by a relative error of at most 0.0075.
Values may be sent and summed in bfloat16 or wider, within the bound.
No kernel may reach another device: no remote copies, remote signals or barrier semaphores. Data moves between devices by JAX's collectives and lax.ppermute only.
A program may use at most 128 MiB of HBM per device.

```python
import jax
import jax.numpy as jnp
from jax import lax

P_SIZE = 128
NT = 316
NEAR = 8
BD = 512
BP = 64
GC = 256
GP = 32
NB = 65536
NPAR = 8192
N_ROW = 8
N_COL = 16


def distinct_prefix(key, leading, pool, taken):
    scores = jax.random.randint(key, leading + (pool,), 0, 1 << 20)
    scores = scores * pool + jnp.arange(pool, dtype=jnp.int32)
    return jnp.argsort(scores, axis=-1)[..., :taken].astype(jnp.int32)


def presence(key, box_total, per_device):
    key_level, key_present = jax.random.split(key, 2)
    devices = box_total // per_device
    level = jax.random.randint(key_level, (devices,), 2, 7)
    owner_level = jnp.repeat(level, per_device)[:, None]
    return jax.random.randint(key_present, (box_total, NT), 0, 10) < owner_level


def draw_leaf_ghosts(key, part):
    key = jax.random.fold_in(key, 11)
    devices = N_ROW * N_COL
    return distinct_prefix(key, (devices, 2 * NEAR), BD, GC)


def draw_parent_ghosts(key, part):
    key = jax.random.fold_in(key, 12)
    devices = N_ROW * N_COL
    return distinct_prefix(key, (devices, N_COL), BP, GP)


def draw_leaf_lists(key, part):
    key = jax.random.fold_in(key, 13)
    key_base, key_kind, key_local, key_first, key_second, key_sign, key_slot = jax.random.split(key, 7)
    devices = N_ROW * N_COL
    present = presence(key_base, NB, BD)
    shape = (NB, NT)
    kind = jax.random.randint(key_kind, shape, 0, 2)
    local = jax.random.randint(key_local, shape, 0, BD)
    first = jax.random.randint(key_first, shape, 0, NEAR)
    second = jax.random.randint(key_second, shape, 0, NEAR)
    magnitude = jnp.minimum(first, second) + 1
    upward = jax.random.randint(key_sign, shape, 0, 2) == 0
    owner = (jnp.arange(NB, dtype=jnp.int32) // BD)[:, None]
    up_valid = owner - magnitude >= 0
    down_valid = owner + magnitude <= devices - 1
    upward = jnp.where(upward, up_valid, jnp.logical_not(down_valid))
    which = jnp.where(upward, magnitude - 1, NEAR + magnitude - 1)
    slot = jax.random.randint(key_slot, shape, 0, GC)
    ghost = BD + which * GC + slot
    return jnp.where(present, jnp.where(kind == 0, local, ghost), -1).astype(jnp.int32)


def draw_parent_lists(key, part):
    key = jax.random.fold_in(key, 14)
    key_base, key_kind, key_local, key_ghost = jax.random.split(key, 4)
    present = presence(key_base, NPAR, BP)
    kind = jax.random.randint(key_kind, (NPAR, NT), 0, 2)
    local = jax.random.randint(key_local, (NPAR, NT), 0, BP)
    ghost = BP + jax.random.randint(key_ghost, (NPAR, NT), 0, N_COL * GP)
    return jnp.where(present, jnp.where(kind == 0, local, ghost), -1).astype(jnp.int32)


def level_of(own_key, shape, cuts, least, high):
    level, own = 1.0, jax.random.fold_in(own_key, 6)
    for axis_at, parts in cuts:
        draws = jnp.exp(jax.random.uniform(jax.random.fold_in(own, axis_at), (parts,), jnp.float32, least / len(cuts), high / len(cuts)))
        level = level * jnp.repeat(draws, shape[axis_at] // parts).reshape([-1 if axis == axis_at else 1 for axis in range(len(shape))])
    return level


def noise(own_key, shape, deviation, limit, cuts=(), held_as=jnp.bfloat16):
    drawn = deviation * jax.random.normal(own_key, shape, jnp.float32)
    if cuts:
        drawn = drawn * level_of(own_key, shape, cuts, -0.22, 0.18)
    return jnp.clip(drawn, -limit, limit).astype(held_as)


def setup_inputs(seed: int = 0) -> dict:
    key_list = jax.random.split(jax.random.key(seed), 10)
    leaf_up = noise(key_list[0], (NB, 3, P_SIZE), 1.0, 6.0, ((0, 128),))
    child_to_parent = noise(key_list[1], (8, P_SIZE, P_SIZE), (8 * P_SIZE) ** -0.5, 0.1875)
    translations = noise(key_list[2], (NT, P_SIZE, P_SIZE), (P_SIZE * NT // 2) ** -0.5, 0.0390625)
    parent_to_child = noise(key_list[3], (8, P_SIZE, P_SIZE), P_SIZE ** -0.5, 0.5)
    check_to_density = noise(key_list[4], (P_SIZE, P_SIZE), (2 * P_SIZE) ** -0.5, 0.375)
    leaf_lists = draw_leaf_lists(jax.random.fold_in(key_list[9], 71), 0)
    leaf_ghosts = draw_leaf_ghosts(jax.random.fold_in(key_list[9], 71), 0)
    parent_lists = draw_parent_lists(jax.random.fold_in(key_list[9], 71), 0)
    parent_ghosts = draw_parent_ghosts(jax.random.fold_in(key_list[9], 71), 0)
    return dict(leaf_up=leaf_up, child_to_parent=child_to_parent, translations=translations, parent_to_child=parent_to_child, check_to_density=check_to_density, leaf_lists=leaf_lists, leaf_ghosts=leaf_ghosts, parent_lists=parent_lists, parent_ghosts=parent_ghosts)


def translate(sources, position, table):
    box_count = position.shape[0]
    block = min(box_count, 128)
    points = table.shape[-1]
    groups = 4
    per_group = table.shape[0] // groups
    padded = jnp.concatenate([sources, jnp.zeros((1, 3, points), sources.dtype)], axis=0)
    chosen = jnp.where(position < 0, sources.shape[0], position).astype(jnp.int32)
    chosen = chosen.reshape(box_count // block, block, groups, per_group).transpose(0, 2, 1, 3)
    grouped_table = table.astype(jnp.float32).reshape(groups, per_group, points, points)

    def per_block(indices):
        def step(total, item):
            picked, operators = item
            gathered = padded[picked].astype(jnp.float32)
            return total + jnp.einsum('btkp,tqp->bkq', gathered, operators), None

        total, _ = lax.scan(step, jnp.zeros((block, 3, points), jnp.float32), (indices, grouped_table))
        return total

    return lax.map(per_block, chosen).reshape(box_count, 3, points)


def reference(leaf_up, child_to_parent, translations, parent_to_child, check_to_density, leaf_lists, leaf_ghosts, parent_lists, parent_ghosts):
    points = leaf_up.shape[-1]
    grouped = leaf_up.astype(jnp.float32).reshape(NPAR, 8, 3, points)
    parent_up = jnp.einsum('bckp,cqp->bkq', grouped, child_to_parent.astype(jnp.float32)).astype(jnp.bfloat16)

    device_total = N_ROW * N_COL
    leaf_owner = (jnp.arange(NB, dtype=jnp.int32) // BD)[:, None]
    offset = jnp.maximum(leaf_lists - BD, 0)
    which = (offset // GC).astype(jnp.int32)
    distance = jnp.where(which < NEAR, which + 1, -(which - NEAR + 1)).astype(jnp.int32)
    sender = jnp.clip(leaf_owner - distance, 0, device_total - 1).astype(jnp.int32)
    ghost_leaf = sender * BD + leaf_ghosts[sender, which, offset % GC]
    leaf_source = jnp.where(leaf_lists < 0, -1, jnp.where(leaf_lists < BD, leaf_owner * BD + leaf_lists, ghost_leaf)).astype(jnp.int32)

    parent_owner = (jnp.arange(NPAR, dtype=jnp.int32) // BP)[:, None]
    owner_row = parent_owner // N_COL
    owner_col = parent_owner % N_COL
    poffset = jnp.maximum(parent_lists - BP, 0)
    psender = owner_row * N_COL + poffset // GP
    ghost_parent = psender * BP + parent_ghosts[psender, owner_col, poffset % GP]
    parent_source = jnp.where(parent_lists < 0, -1, jnp.where(parent_lists < BP, parent_owner * BP + parent_lists, ghost_parent)).astype(jnp.int32)

    inverse = check_to_density.astype(jnp.float32)
    parent_check = translate(parent_up, parent_source, translations).astype(jnp.bfloat16)
    parent_down = jnp.einsum('bkp,qp->bkq', parent_check.astype(jnp.float32), inverse).astype(jnp.bfloat16)
    from_parent = jnp.einsum('bkp,cqp->bckq', parent_down.astype(jnp.float32), parent_to_child.astype(jnp.float32)).reshape(NB, 3, points)
    leaf_check = (from_parent + translate(leaf_up, leaf_source, translations)).astype(jnp.bfloat16)
    return jnp.einsum('bkp,qp->bkq', leaf_check.astype(jnp.float32), inverse).astype(jnp.bfloat16)
```

```python
import jax
import jax.numpy as jnp
from jax import lax
from jax.experimental import pallas as pl
from jax.experimental.pallas import tpu as pltpu
from jax.sharding import PartitionSpec as P

RING = 4
VMEM_BYTES = 58 * 2**20


def dot_nt(left, right):
    return lax.dot_general(
        left, right, (((1,), (1,)), ((), ())), preferred_element_type=jnp.float32
    )


def pick_pair(table, low_half, first, second):
    upper = table[pl.ds(first + 4, 8), :]
    lower = table[pl.ds(second, 8), :]
    return jnp.where(low_half, upper, lower)


def prepare_kernel(
    planes_ref, ghosts_ref, parent_ghosts_ref, operators_ref, *refs, offsets, slots, columns, parent_slots
):
    outgoing = refs[:offsets]
    parent_ref, parent_sent_ref, table, parent_table, gathered, parent_gathered = refs[offsets:]
    boxes = planes_ref.shape[1]
    parents = parent_ref.shape[1]
    low_half = lax.broadcasted_iota(jnp.int32, (8, 128), 0) < 4
    for k in range(3):
        table[pl.ds(4 + k, boxes, stride=4), :] = planes_ref[k].astype(jnp.float32)
    operators = jnp.concatenate([operators_ref[c] for c in range(8)], axis=1)
    for k in range(3):
        children = jnp.concatenate(
            [table[pl.ds(4 + 4 * c + k, parents, stride=32), :] for c in range(8)], axis=1
        ).astype(jnp.bfloat16)
        rounded = dot_nt(children, operators).astype(jnp.bfloat16)
        parent_ref[k] = rounded
        parent_table[pl.ds(4 + k, parents, stride=4), :] = rounded.astype(jnp.float32)
    for column in range(columns):
        for pair in range(parent_slots // 2):
            at = column * parent_slots + 2 * pair
            parent_gathered[8 * pair : 8 * pair + 8, :] = pick_pair(
                parent_table, low_half, parent_ghosts_ref[0, at], parent_ghosts_ref[0, at + 1]
            )
        for k in range(3):
            parent_sent_ref[column, k] = parent_gathered[
                pl.ds(k, parent_slots, stride=4), :
            ].astype(jnp.bfloat16)
    for which in range(offsets):
        for pair in range(slots // 2):
            at = which * slots + 2 * pair
            gathered[8 * pair : 8 * pair + 8, :] = pick_pair(
                table, low_half, ghosts_ref[0, at], ghosts_ref[0, at + 1]
            )
        for k in range(3):
            outgoing[which][k] = gathered[pl.ds(k, slots, stride=4), :].astype(jnp.bfloat16)


def prepare(planes, ghosts, parent_ghosts, operators):
    boxes = planes.shape[1]
    parents = boxes // 8
    offsets, slots = ghosts.shape
    columns, parent_slots = parent_ghosts.shape
    vmem = pl.BlockSpec(memory_space=pltpu.VMEM)
    smem = pl.BlockSpec(memory_space=pltpu.SMEM)

    def kernel(*refs):
        prepare_kernel(
            *refs, offsets=offsets, slots=slots, columns=columns, parent_slots=parent_slots
        )

    out = pl.pallas_call(
        kernel,
        in_specs=[vmem, smem, smem, vmem],
        out_specs=[vmem] * (offsets + 2),
        out_shape=[jax.ShapeDtypeStruct((3, slots, 128), jnp.bfloat16)] * offsets
        + [
            jax.ShapeDtypeStruct((3, parents, 128), jnp.bfloat16),
            jax.ShapeDtypeStruct((columns, 3, parent_slots, 128), jnp.bfloat16),
        ],
        scratch_shapes=[
            pltpu.VMEM((4 * boxes + 16, 128), jnp.float32),
            pltpu.VMEM((4 * parents + 16, 128), jnp.float32),
            pltpu.VMEM((4 * slots, 128), jnp.float32),
            pltpu.VMEM((4 * parent_slots, 128), jnp.float32),
        ],
        compiler_params=pltpu.CompilerParams(vmem_limit_bytes=VMEM_BYTES),
        name="prepare",
    )(
        planes,
        (ghosts * 4).reshape(1, -1),
        (parent_ghosts * 4).reshape(1, -1),
        operators,
    )
    return out[:offsets], out[offsets], out[offsets + 1]


def order_lists(lists, block, group):
    boxes, vectors = lists.shape
    places = (lists + 1) * 4
    places = places.T.reshape(vectors // group, group, boxes // block, block)
    places = places.transpose(0, 2, 1, 3).reshape(-1, 1, group * block)
    steps = places.shape[0]
    padding = -steps % RING + RING
    return jnp.concatenate(
        [places, jnp.zeros((padding, 1, group * block), places.dtype)], axis=0
    )


def translate_steps(lists_hbm, table, operators, total, chunk, chunk_sem, block, group):
    blocks = total.shape[0]
    groups = operators.shape[0] // group
    steps = lists_hbm.shape[0] - RING
    low_half = lax.broadcasted_iota(jnp.int32, (8, 128), 0) < 4

    def fetch(step, slot):
        return pltpu.make_async_copy(lists_hbm.at[step], chunk.at[slot], chunk_sem.at[slot])

    def round_of_steps(turn, _):
        for slot in range(RING):
            step = turn * RING + slot
            fetch(step, slot).wait()
            which = jnp.minimum(step // blocks, groups - 1)
            target = step % blocks
            columns = []
            for t in range(group):
                rows = []
                for pair in range(block // 2):
                    at = t * block + 2 * pair
                    rows.append(
                        pick_pair(table, low_half, chunk[slot, 0, at], chunk[slot, 0, at + 1])
                    )
                columns.append(jnp.concatenate(rows, axis=0).astype(jnp.bfloat16))
            sources = jnp.concatenate(columns, axis=1)
            matrices = jnp.concatenate(
                [operators[which * group + t] for t in range(group)], axis=1
            )
            total[target] += dot_nt(sources, matrices)
            fetch(step + RING, slot).start()
        return 0

    lax.fori_loop(0, steps // RING, round_of_steps, 0)
    for slot in range(RING):
        fetch(steps + slot, slot).wait()


def first_fetches(lists_hbm, chunk, chunk_sem):
    for slot in range(RING):
        pltpu.make_async_copy(lists_hbm.at[slot], chunk.at[slot], chunk_sem.at[slot]).start()


def parent_level(own, came, lists, translations, inverse, block, group):
    parents = own.shape[1]
    columns, _, slots, _ = came.shape
    count = parents + columns * slots

    def kernel(
        own_ref, came_ref, lists_hbm, operators_ref, inverse_ref, out_ref,
        table, total, result, chunk, chunk_sem,
    ):
        first_fetches(lists_hbm, chunk, chunk_sem)
        table[...] = jnp.zeros_like(table)
        total[...] = jnp.zeros_like(total)
        for k in range(3):
            table[pl.ds(8 + k, parents, stride=4), :] = own_ref[k].astype(jnp.float32)
            for column in range(columns):
                at = 8 + k + 4 * (parents + column * slots)
                table[pl.ds(at, slots, stride=4), :] = came_ref[column, k].astype(jnp.float32)
        translate_steps(
            lists_hbm, table, operators_ref, total, chunk, chunk_sem, block, group
        )
        check = total[...].reshape(4 * parents, 128).astype(jnp.bfloat16)
        result[...] = dot_nt(check, inverse_ref[...])
        for k in range(3):
            out_ref[k] = result[pl.ds(k, parents, stride=4), :].astype(jnp.bfloat16)

    vmem = pl.BlockSpec(memory_space=pltpu.VMEM)
    hbm = pl.BlockSpec(memory_space=pl.ANY)
    return pl.pallas_call(
        kernel,
        in_specs=[vmem, vmem, hbm, vmem, vmem],
        out_specs=vmem,
        out_shape=jax.ShapeDtypeStruct((3, parents, 128), jnp.bfloat16),
        scratch_shapes=[
            pltpu.VMEM((4 * count + 16, 128), jnp.float32),
            pltpu.VMEM((parents // block, 4 * block, 128), jnp.float32),
            pltpu.VMEM((4 * parents, 128), jnp.float32),
            pltpu.SMEM((RING, 1, block * group), jnp.int32),
            pltpu.SemaphoreType.DMA((RING,)),
        ],
        compiler_params=pltpu.CompilerParams(vmem_limit_bytes=VMEM_BYTES),
        name="parent_level",
    )(own, came, lists, translations, inverse)


def leaf_level(own, arrived, parent_down, lists, translations, to_child, inverse, block, group):
    boxes = own.shape[1]
    parents = boxes // 8
    offsets = len(arrived)
    slots = arrived[0].shape[1]
    count = boxes + offsets * slots

    def kernel(*refs):
        own_ref, parent_ref, lists_hbm, operators_hbm, to_child_ref, inverse_ref = refs[:6]
        ghost_hbm = refs[6 : 6 + offsets]
        (
            out_ref, table, operators, ghosts, total, result, chunk, chunk_sem, operator_sem,
            ghost_sem,
        ) = refs[6 + offsets :]
        ghost_copies = [
            pltpu.make_async_copy(ghost_hbm[j], ghosts.at[j], ghost_sem.at[j])
            for j in range(offsets)
        ]
        for copy in ghost_copies:
            copy.start()
        operator_copy = pltpu.make_async_copy(operators_hbm, operators, operator_sem)
        operator_copy.start()
        first_fetches(lists_hbm, chunk, chunk_sem)
        low_rows = jnp.zeros((8, 128), jnp.float32)
        table[0:8, :] = low_rows
        table[pl.ds(8 + 3, count, stride=4), :] = jnp.zeros((count, 128), jnp.float32)
        for k in range(3):
            table[pl.ds(8 + k, boxes, stride=4), :] = own_ref[k].astype(jnp.float32)
        result[...] = jnp.zeros_like(result)
        for c in range(8):
            for k in range(3):
                result[pl.ds(4 * c + k, parents, stride=32), :] = dot_nt(
                    parent_ref[k], to_child_ref[c]
                )
        for b in range(boxes // block):
            total[b] = result[4 * block * b : 4 * block * (b + 1), :]
        for j in range(offsets):
            ghost_copies[j].wait()
            for k in range(3):
                at = 8 + k + 4 * (boxes + j * slots)
                table[pl.ds(at, slots, stride=4), :] = ghosts[j, k].astype(jnp.float32)
        operator_copy.wait()
        translate_steps(lists_hbm, table, operators, total, chunk, chunk_sem, block, group)
        for b in range(boxes // block):
            result[4 * block * b : 4 * block * (b + 1), :] = dot_nt(
                total[b].astype(jnp.bfloat16), inverse_ref[...]
            )
        for k in range(3):
            out_ref[k] = result[pl.ds(k, boxes, stride=4), :].astype(jnp.bfloat16)

    vmem = pl.BlockSpec(memory_space=pltpu.VMEM)
    hbm = pl.BlockSpec(memory_space=pl.ANY)
    return pl.pallas_call(
        kernel,
        in_specs=[vmem, vmem, hbm, hbm, vmem, vmem] + [hbm] * offsets,
        out_specs=vmem,
        out_shape=jax.ShapeDtypeStruct((3, boxes, 128), jnp.bfloat16),
        scratch_shapes=[
            pltpu.VMEM((4 * count + 16, 128), jnp.float32),
            pltpu.VMEM(translations.shape, translations.dtype),
            pltpu.VMEM((offsets, 3, slots, 128), jnp.bfloat16),
            pltpu.VMEM((boxes // block, 4 * block, 128), jnp.float32),
            pltpu.VMEM((4 * boxes, 128), jnp.float32),
            pltpu.SMEM((RING, 1, block * group), jnp.int32),
            pltpu.SemaphoreType.DMA((RING,)),
            pltpu.SemaphoreType.DMA,
            pltpu.SemaphoreType.DMA((offsets,)),
        ],
        compiler_params=pltpu.CompilerParams(vmem_limit_bytes=VMEM_BYTES),
        name="leaf_level",
    )(own, parent_down, lists, translations, to_child, inverse, *arrived)


def from_behind(value, axis, steps):
    count = lax.axis_size(axis)
    first, last = (max(0, -steps), min(count, count - steps))
    return lax.ppermute(value, axis, [(source, source + steps) for source in range(first, last)])


def rank_distance(which, near_count):
    if which < near_count:
        return which + 1
    return -(which - near_count + 1)


def local(
    leaf_up,
    child_to_parent,
    translations,
    parent_to_child,
    check_to_density,
    leaf_lists,
    leaf_ghosts,
    parent_lists,
    parent_ghosts,
):
    planes = leaf_up.transpose(1, 0, 2)
    outgoing, parent_up, parent_sent = prepare(
        planes, leaf_ghosts[0], parent_ghosts[0], child_to_parent
    )
    near_count = len(outgoing) // 2
    parent_came = lax.all_to_all(parent_sent, "col", split_axis=0, concat_axis=0, tiled=True)
    arrived = [None] * len(outgoing)
    for distance in range(near_count):
        for which in (distance, distance + near_count):
            arrived[which] = from_behind(
                outgoing[which], ("row", "col"), rank_distance(which, near_count)
            )
    parent_down = parent_level(
        parent_up,
        parent_came,
        order_lists(parent_lists, 64, 4),
        translations,
        check_to_density,
        64,
        4,
    )
    leaf_down = leaf_level(
        planes,
        arrived,
        parent_down,
        order_lists(leaf_lists, 128, 4),
        translations,
        parent_to_child,
        check_to_density,
        128,
        4,
    )
    return leaf_down.transpose(1, 0, 2)


def solution(mesh):
    return jax.shard_map(
        local,
        mesh=mesh,
        in_specs=(
            P(("row", "col"), None, None),
            P(),
            P(),
            P(),
            P(),
            P(("row", "col"), None),
            P(("row", "col"), None, None),
            P(("row", "col"), None),
            P(("row", "col"), None, None),
        ),
        out_specs=P(("row", "col"), None, None),
        check_vma=False,
    )
```

```python
import jax
import jax.numpy as jnp
from jax import lax
from jax.experimental import pallas as pl
from jax.experimental.pallas import tpu as pltpu
from jax.sharding import PartitionSpec as P

RING = 2
NEAR = 8
VMEM_BYTES = 58 * 2**20


def dot_nt(left, right):
    return lax.dot_general(
        left, right, (((1,), (1,)), ((), ())), preferred_element_type=jnp.float32
    )


def pick_pair(table, low_half, first, second):
    upper = table[pl.ds(first + 4, 8), :]
    lower = table[pl.ds(second, 8), :]
    return jnp.where(low_half, upper, lower)


def spread(table, at, planes_ref):
    for k in range(3):
        plane = planes_ref[k]
        table[pl.ds(at + k, plane.shape[0], stride=4), :] = plane.astype(jnp.float32)


def select_rows(table, places_ref, start, count, gathered, out_ref):
    low_half = lax.broadcasted_iota(jnp.int32, (8, 128), 0) < 4
    for pair in range(count // 2):
        at = start + 2 * pair
        gathered[8 * pair : 8 * pair + 8, :] = pick_pair(
            table, low_half, places_ref[0, at], places_ref[0, at + 1]
        )
    for k in range(3):
        out_ref[k] = gathered[pl.ds(k, count, stride=4), :].astype(jnp.bfloat16)


def raise_parents(planes, ghosts, operators):
    boxes = planes.shape[1]
    parents = boxes // 8
    columns, slots = ghosts.shape

    def kernel(
        planes_ref, ghosts_ref, operators_ref, up_ref, sent_ref, zero_ref, table, own, gathered
    ):
        zero_ref[0, 0] = 0
        spread(table, 0, planes_ref)
        matrices = jnp.concatenate([operators_ref[c] for c in range(8)], axis=1)
        for k in range(3):
            children = jnp.concatenate(
                [table[pl.ds(4 * c + k, parents, stride=32), :] for c in range(8)], axis=1
            )
            up_ref[k] = dot_nt(children.astype(jnp.bfloat16), matrices).astype(jnp.bfloat16)
        spread(own, 4, up_ref)
        for column in range(columns):
            select_rows(own, ghosts_ref, column * slots, slots, gathered, sent_ref.at[column])

    vmem = pl.BlockSpec(memory_space=pltpu.VMEM)
    return pl.pallas_call(
        kernel,
        in_specs=[vmem, pl.BlockSpec(memory_space=pltpu.SMEM), vmem],
        out_specs=[vmem, vmem, pl.BlockSpec(memory_space=pltpu.SMEM)],
        out_shape=[
            jax.ShapeDtypeStruct((3, parents, 128), jnp.bfloat16),
            jax.ShapeDtypeStruct((columns, 3, slots, 128), jnp.bfloat16),
            jax.ShapeDtypeStruct((1, 1), jnp.int32),
        ],
        scratch_shapes=[
            pltpu.VMEM((4 * boxes, 128), jnp.float32),
            pltpu.VMEM((4 * parents + 16, 128), jnp.float32),
            pltpu.VMEM((4 * slots, 128), jnp.float32),
        ],
        compiler_params=pltpu.CompilerParams(vmem_limit_bytes=VMEM_BYTES),
        name="raise_parents",
    )(planes, (ghosts * 4).reshape(1, -1), operators)


def select_leaves(planes, ghosts):
    boxes = planes.shape[1]
    messages, slots = ghosts.shape

    def kernel(planes_ref, ghosts_ref, sent_ref, direct_ref, table, gathered):
        spread(table, 4, planes_ref)
        for which in range(messages):
            target = direct_ref if which == messages - 1 else sent_ref.at[which]
            select_rows(table, ghosts_ref, which * slots, slots, gathered, target)

    vmem = pl.BlockSpec(memory_space=pltpu.VMEM)
    return pl.pallas_call(
        kernel,
        in_specs=[vmem, pl.BlockSpec(memory_space=pltpu.SMEM)],
        out_specs=[vmem, vmem],
        out_shape=[
            jax.ShapeDtypeStruct((messages - 1, 3, slots, 128), jnp.bfloat16),
            jax.ShapeDtypeStruct((3, slots, 128), jnp.bfloat16),
        ],
        scratch_shapes=[
            pltpu.VMEM((4 * boxes + 16, 128), jnp.float32),
            pltpu.VMEM((4 * slots, 128), jnp.float32),
        ],
        compiler_params=pltpu.CompilerParams(vmem_limit_bytes=VMEM_BYTES),
        name="select_leaves",
    )(planes, (ghosts * 4).reshape(1, -1))


def order_lists(lists, block, group, chunk_steps):
    boxes, vectors = lists.shape
    places = (lists + 1) * 4
    places = places.T.reshape(vectors // group, group, boxes // block, block)
    places = places.transpose(0, 2, 1, 3).reshape(-1, group * block)
    padding = -places.shape[0] % (RING * chunk_steps) + RING * chunk_steps
    places = jnp.concatenate(
        [places, jnp.zeros((padding, group * block), places.dtype)], axis=0
    )
    return places.reshape(-1, 1, chunk_steps * group * block)


def translate_steps(
    lists_hbm, table, operators, total, chunk, chunk_sem, block, group, chunk_steps, at_turn
):
    blocks = total.shape[0]
    groups = operators.shape[0] // group
    chunks = lists_hbm.shape[0] - RING
    size = block * group
    low_half = lax.broadcasted_iota(jnp.int32, (8, 128), 0) < 4

    def fetch(at, slot):
        return pltpu.make_async_copy(lists_hbm.at[at], chunk.at[slot], chunk_sem.at[slot])

    def round_of_chunks(turn, _):
        at_turn(turn)
        for slot in range(RING):
            fetch(turn * RING + slot, slot).wait()
            for h in range(chunk_steps):
                which = ((turn * RING + slot) * chunk_steps + h) // blocks
                which = jnp.minimum(which, groups - 1)
                columns = []
                for t in range(group):
                    rows = []
                    for pair in range(block // 2):
                        at = h * size + t * block + 2 * pair
                        rows.append(
                            pick_pair(table, low_half, chunk[slot, 0, at], chunk[slot, 0, at + 1])
                        )
                    columns.append(jnp.concatenate(rows, axis=0).astype(jnp.bfloat16))
                sources = jnp.concatenate(columns, axis=1)
                matrices = jnp.concatenate(
                    [operators[which * group + t] for t in range(group)], axis=1
                )
                total[h % blocks] += dot_nt(sources, matrices)
            fetch((turn + 1) * RING + slot, slot).start()
        return 0

    lax.fori_loop(0, chunks // RING, round_of_chunks, 0)
    for slot in range(RING):
        fetch(chunks + slot, slot).wait()


def split_operator_copy(operators_hbm, operators, sems, first):
    return (
        pltpu.make_async_copy(
            operators_hbm.at[pl.ds(0, first)], operators.at[pl.ds(0, first)], sems.at[0]
        ),
        pltpu.make_async_copy(
            operators_hbm.at[pl.ds(first, operators.shape[0] - first)],
            operators.at[pl.ds(first, operators.shape[0] - first)],
            sems.at[1],
        ),
    )


def first_fetches(lists_hbm, chunk, chunk_sem):
    for slot in range(RING):
        pltpu.make_async_copy(lists_hbm.at[slot], chunk.at[slot], chunk_sem.at[slot]).start()


def parent_level(own, came, lists, translations, inverse, block, group, chunk_steps):
    parents = own.shape[1]
    columns, _, slots, _ = came.shape
    count = parents + columns * slots
    first = RING * chunk_steps * group

    def kernel(
        own_ref, came_ref, lists_hbm, operators_hbm, inverse_ref, out_ref,
        table, operators, total, result, chunk, chunk_sem, operator_sem,
    ):
        early, late = split_operator_copy(operators_hbm, operators, operator_sem, first)
        early.start()
        first_fetches(lists_hbm, chunk, chunk_sem)
        late.start()
        table[...] = jnp.zeros_like(table)
        total[...] = jnp.zeros_like(total)
        spread(table, 8, own_ref)
        for column in range(columns):
            spread(table, 8 + 4 * (parents + column * slots), came_ref.at[column])
        early.wait()

        def at_turn(turn):
            pl.when(turn == 1)(lambda: late.wait())

        translate_steps(
            lists_hbm, table, operators, total, chunk, chunk_sem, block, group, chunk_steps,
            at_turn,
        )
        check = total[...].reshape(4 * parents, 128).astype(jnp.bfloat16)
        result[...] = dot_nt(check, inverse_ref[...])
        for k in range(3):
            out_ref[k] = result[pl.ds(k, parents, stride=4), :].astype(jnp.bfloat16)

    vmem = pl.BlockSpec(memory_space=pltpu.VMEM)
    hbm = pl.BlockSpec(memory_space=pl.ANY)
    return pl.pallas_call(
        kernel,
        in_specs=[vmem, vmem, hbm, hbm, vmem],
        out_specs=vmem,
        out_shape=jax.ShapeDtypeStruct((3, parents, 128), jnp.bfloat16),
        scratch_shapes=[
            pltpu.VMEM((4 * count + 16, 128), jnp.float32),
            pltpu.VMEM(translations.shape, translations.dtype),
            pltpu.VMEM((parents // block, 4 * block, 128), jnp.float32),
            pltpu.VMEM((4 * parents, 128), jnp.float32),
            pltpu.SMEM((RING, 1, chunk_steps * block * group), jnp.int32),
            pltpu.SemaphoreType.DMA((RING,)),
            pltpu.SemaphoreType.DMA((2,)),
        ],
        compiler_params=pltpu.CompilerParams(vmem_limit_bytes=VMEM_BYTES),
        name="parent_level",
    )(own, came, lists, translations, inverse)


def leaf_level(
    own, came, shifted, direct, origin, parent_down, lists, translations, to_child, inverse,
    block, group, chunk_steps,
):
    boxes = own.shape[1]
    parents = boxes // 8
    offsets = origin.shape[1]
    slots = direct.shape[1]
    count = boxes + offsets * slots
    first = RING * chunk_steps * group // (boxes // block)

    def kernel(
        origin_ref, own_ref, parent_ref, to_child_ref, inverse_ref, lists_hbm, operators_hbm,
        came_hbm, shifted_hbm, direct_hbm, out_ref,
        table, operators, ghosts, total, result, chunk, chunk_sem, operator_sem, ghost_sem,
    ):
        def ghost_copy(source, j):
            return pltpu.make_async_copy(source, ghosts.at[j], ghost_sem.at[j])

        for j in range(offsets):
            kind, place = origin_ref[0, j], origin_ref[1, j]
            pl.when(kind == 0)(lambda: ghost_copy(came_hbm.at[place], j).start())
            pl.when(kind == 1)(lambda: ghost_copy(shifted_hbm.at[place], j).start())
            pl.when(kind == 2)(lambda: ghost_copy(direct_hbm, j).start())
        first_fetches(lists_hbm, chunk, chunk_sem)
        early, late = split_operator_copy(operators_hbm, operators, operator_sem, first)
        early.start()
        late.start()
        table[0:8, :] = jnp.zeros((8, 128), jnp.float32)
        table[pl.ds(8 + 3, count, stride=4), :] = jnp.zeros((count, 128), jnp.float32)
        spread(table, 8, own_ref)
        result[pl.ds(3, boxes, stride=4), :] = jnp.zeros((boxes, 128), jnp.float32)
        for c in range(8):
            for k in range(3):
                result[pl.ds(4 * c + k, parents, stride=32), :] = dot_nt(
                    parent_ref[k], to_child_ref[c]
                )
        for b in range(boxes // block):
            total[b] = result[4 * block * b : 4 * block * (b + 1), :]
        for j in range(offsets):
            ghost_copy(direct_hbm, j).wait()
            spread(table, 8 + 4 * (boxes + j * slots), ghosts.at[j])
        early.wait()

        def at_turn(turn):
            pl.when(turn == 1)(lambda: late.wait())

        translate_steps(
            lists_hbm, table, operators, total, chunk, chunk_sem, block, group, chunk_steps,
            at_turn,
        )
        for b in range(boxes // block):
            result[4 * block * b : 4 * block * (b + 1), :] = dot_nt(
                total[b].astype(jnp.bfloat16), inverse_ref[...]
            )
        for k in range(3):
            out_ref[k] = result[pl.ds(k, boxes, stride=4), :].astype(jnp.bfloat16)

    vmem = pl.BlockSpec(memory_space=pltpu.VMEM)
    smem = pl.BlockSpec(memory_space=pltpu.SMEM)
    hbm = pl.BlockSpec(memory_space=pl.ANY)
    return pl.pallas_call(
        kernel,
        in_specs=[smem, vmem, vmem, vmem, vmem, hbm, hbm, hbm, hbm, hbm],
        out_specs=vmem,
        out_shape=jax.ShapeDtypeStruct((3, boxes, 128), jnp.bfloat16),
        scratch_shapes=[
            pltpu.VMEM((4 * count + 16, 128), jnp.float32),
            pltpu.VMEM(translations.shape, translations.dtype),
            pltpu.VMEM((offsets, 3, slots, 128), jnp.bfloat16),
            pltpu.VMEM((boxes // block, 4 * block, 128), jnp.float32),
            pltpu.VMEM((4 * boxes, 128), jnp.float32),
            pltpu.SMEM((RING, 1, chunk_steps * block * group), jnp.int32),
            pltpu.SemaphoreType.DMA((RING,)),
            pltpu.SemaphoreType.DMA((2,)),
            pltpu.SemaphoreType.DMA((offsets,)),
        ],
        compiler_params=pltpu.CompilerParams(vmem_limit_bytes=VMEM_BYTES),
        name="leaf_level",
    )(
        origin, own, parent_down, to_child, inverse, lists, translations, came, shifted, direct
    )


def offset_index(distance):
    return jnp.where(distance > 0, distance - 1, NEAR - 1 - distance)


def message_order(column, columns):
    difference = jnp.arange(columns) - column
    distance = jnp.where(difference > NEAR, difference - columns, difference)
    distance = jnp.where(distance < -NEAR, distance + columns, distance)
    order = jnp.where(distance == 0, 0, offset_index(distance))
    last = offset_index(jnp.where(column < NEAR, -NEAR, NEAR))
    return jnp.concatenate([order, last[None]])


def message_origin(column, columns):
    offset = jnp.arange(2 * NEAR)
    distance = jnp.where(offset < NEAR, offset + 1, NEAR - 1 - offset)
    sender = column - distance
    inside = (sender >= 0) & (sender < columns)
    direct = jnp.abs(distance) == NEAR
    kind = jnp.where(inside, 0, jnp.where(direct, 2, 1))
    turned = jnp.where(sender < 0, sender + NEAR - 1, sender - columns)
    place = jnp.where(inside, sender, jnp.where(direct, 0, turned))
    return jnp.stack([kind, place]).astype(jnp.int32)


def local(
    leaf_up,
    child_to_parent,
    translations,
    parent_to_child,
    check_to_density,
    leaf_lists,
    leaf_ghosts,
    parent_lists,
    parent_ghosts,
):
    rows, columns = lax.axis_size("row"), lax.axis_size("col")
    column = lax.axis_index("col")
    planes = leaf_up.transpose(1, 0, 2)
    parent_up, parent_sent, zero = raise_parents(planes, parent_ghosts[0], child_to_parent)
    parent_came = lax.all_to_all(parent_sent, "col", split_axis=0, concat_axis=0, tiled=True)
    chosen = leaf_ghosts[0][message_order(column, columns)] + zero
    sent, direct = select_leaves(planes, chosen)
    came = lax.all_to_all(sent, "col", split_axis=0, concat_axis=0, tiled=True)
    ranks = range(rows * columns)
    half = [(d, d + NEAR if d % columns >= NEAR else d - NEAR) for d in ranks]
    direct = lax.ppermute(direct, ("row", "col"), [p for p in half if p[1] in ranks])
    parent_down = parent_level(
        parent_up,
        parent_came,
        order_lists(parent_lists, 64, 4, 8),
        translations,
        check_to_density,
        64,
        4,
        8,
    )
    lists = order_lists(leaf_lists, 256, 4, 4)
    came, parent_down, lists = lax.optimization_barrier((came, parent_down, lists))
    turn = [(d, d + columns if d % columns < NEAR else d - columns) for d in ranks]
    passing = lax.dynamic_slice_in_dim(came, jnp.where(column < NEAR, NEAR + 1, 0), NEAR - 1)
    shifted = lax.ppermute(passing, ("row", "col"), [p for p in turn if p[1] in ranks])
    leaf_down = leaf_level(
        planes,
        came,
        shifted,
        direct,
        message_origin(column, columns),
        parent_down,
        lists,
        translations,
        parent_to_child,
        check_to_density,
        256,
        4,
        4,
    )
    return leaf_down.transpose(1, 0, 2)


def solution(mesh):
    return jax.shard_map(
        local,
        mesh=mesh,
        in_specs=(
            P(("row", "col"), None, None),
            P(),
            P(),
            P(),
            P(),
            P(("row", "col"), None),
            P(("row", "col"), None, None),
            P(("row", "col"), None),
            P(("row", "col"), None, None),
        ),
        out_specs=P(("row", "col"), None, None),
        check_vma=False,
    )
```

```python
import jax
import jax.numpy as jnp
from jax import lax
from jax.experimental import pallas as pl
from jax.experimental.pallas import tpu as pltpu
from jax.sharding import PartitionSpec as P

RING = 2
NEAR = 8
VMEM_BYTES = 58 * 2**20


def dot_nt(left, right):
    return lax.dot_general(
        left, right, (((1,), (1,)), ((), ())), preferred_element_type=jnp.float32
    )


def pick_pair(table, low_half, first, second):
    upper = table[pl.ds(first + 4, 8), :]
    lower = table[pl.ds(second, 8), :]
    return jnp.where(low_half, upper, lower)


def spread(table, at, planes_ref):
    for k in range(3):
        plane = planes_ref[k]
        table[pl.ds(at + k, plane.shape[0], stride=4), :] = plane.astype(jnp.float32)


def select_rows(table, places_ref, start, count, gathered, out_ref):
    low_half = lax.broadcasted_iota(jnp.int32, (8, 128), 0) < 4
    for pair in range(count // 2):
        at = start + 2 * pair
        gathered[8 * pair : 8 * pair + 8, :] = pick_pair(
            table, low_half, places_ref[0, at], places_ref[0, at + 1]
        )
    for k in range(3):
        out_ref[k] = gathered[pl.ds(k, count, stride=4), :].astype(jnp.bfloat16)


def prepare(planes, ghosts, parent_ghosts, operators):
    boxes = planes.shape[1]
    parents = boxes // 8
    messages, slots = ghosts.shape
    columns, parent_slots = parent_ghosts.shape
    passed = messages - columns - 1

    def kernel(
        planes_ref, ghosts_ref, parent_ghosts_ref, operators_ref,
        sent_ref, passing_ref, direct_ref, up_ref, parent_sent_ref,
        table, own, gathered, parent_gathered,
    ):
        spread(table, 4, planes_ref)
        matrices = jnp.concatenate([operators_ref[c] for c in range(8)], axis=1)
        for k in range(3):
            children = jnp.concatenate(
                [table[pl.ds(4 + 4 * c + k, parents, stride=32), :] for c in range(8)], axis=1
            )
            up_ref[k] = dot_nt(children.astype(jnp.bfloat16), matrices).astype(jnp.bfloat16)
        spread(own, 4, up_ref)
        for column in range(columns):
            select_rows(
                own, parent_ghosts_ref, column * parent_slots, parent_slots, parent_gathered,
                parent_sent_ref.at[column],
            )
        targets = [sent_ref.at[i] for i in range(columns)]
        targets += [passing_ref.at[i] for i in range(passed)] + [direct_ref]
        for which, target in enumerate(targets):
            select_rows(table, ghosts_ref, which * slots, slots, gathered, target)

    vmem = pl.BlockSpec(memory_space=pltpu.VMEM)
    smem = pl.BlockSpec(memory_space=pltpu.SMEM)
    return pl.pallas_call(
        kernel,
        in_specs=[vmem, smem, smem, vmem],
        out_specs=[vmem] * 5,
        out_shape=[
            jax.ShapeDtypeStruct((columns, 3, slots, 128), jnp.bfloat16),
            jax.ShapeDtypeStruct((passed, 3, slots, 128), jnp.bfloat16),
            jax.ShapeDtypeStruct((3, slots, 128), jnp.bfloat16),
            jax.ShapeDtypeStruct((3, parents, 128), jnp.bfloat16),
            jax.ShapeDtypeStruct((columns, 3, parent_slots, 128), jnp.bfloat16),
        ],
        scratch_shapes=[
            pltpu.VMEM((4 * boxes + 16, 128), jnp.float32),
            pltpu.VMEM((4 * parents + 16, 128), jnp.float32),
            pltpu.VMEM((4 * slots, 128), jnp.float32),
            pltpu.VMEM((4 * parent_slots, 128), jnp.float32),
        ],
        compiler_params=pltpu.CompilerParams(vmem_limit_bytes=VMEM_BYTES),
        name="prepare",
    )(
        planes, (ghosts * 4).reshape(1, -1), (parent_ghosts * 4).reshape(1, -1), operators
    )


def order_lists(lists, block, group, chunk_steps):
    boxes, vectors = lists.shape
    places = (lists + 1) * 4
    places = places.T.reshape(vectors // group, group, boxes // block, block)
    places = places.transpose(0, 2, 1, 3).reshape(-1, group * block)
    padding = -places.shape[0] % (RING * chunk_steps) + RING * chunk_steps
    places = jnp.concatenate(
        [places, jnp.zeros((padding, group * block), places.dtype)], axis=0
    )
    return places.reshape(-1, 1, chunk_steps * group * block)


def translate_steps(
    lists_hbm, table, operators, total, chunk, chunk_sem, block, group, chunk_steps, at_turn
):
    blocks = total.shape[0]
    groups = operators.shape[0] // group
    chunks = lists_hbm.shape[0] - RING
    size = block * group
    low_half = lax.broadcasted_iota(jnp.int32, (8, 128), 0) < 4

    def fetch(at, slot):
        return pltpu.make_async_copy(lists_hbm.at[at], chunk.at[slot], chunk_sem.at[slot])

    def round_of_chunks(turn, _):
        at_turn(turn)
        for slot in range(RING):
            fetch(turn * RING + slot, slot).wait()
            for h in range(chunk_steps):
                which = ((turn * RING + slot) * chunk_steps + h) // blocks
                which = jnp.minimum(which, groups - 1)
                columns = []
                for t in range(group):
                    rows = []
                    for pair in range(block // 2):
                        at = h * size + t * block + 2 * pair
                        rows.append(
                            pick_pair(table, low_half, chunk[slot, 0, at], chunk[slot, 0, at + 1])
                        )
                    columns.append(jnp.concatenate(rows, axis=0).astype(jnp.bfloat16))
                sources = jnp.concatenate(columns, axis=1)
                matrices = jnp.concatenate(
                    [operators[which * group + t] for t in range(group)], axis=1
                )
                total[h % blocks] += dot_nt(sources, matrices)
            fetch((turn + 1) * RING + slot, slot).start()
        return 0

    lax.fori_loop(0, chunks // RING, round_of_chunks, 0)
    for slot in range(RING):
        fetch(chunks + slot, slot).wait()


def split_operator_copy(operators_hbm, operators, sems, first):
    return (
        pltpu.make_async_copy(
            operators_hbm.at[pl.ds(0, first)], operators.at[pl.ds(0, first)], sems.at[0]
        ),
        pltpu.make_async_copy(
            operators_hbm.at[pl.ds(first, operators.shape[0] - first)],
            operators.at[pl.ds(first, operators.shape[0] - first)],
            sems.at[1],
        ),
    )


def first_fetches(lists_hbm, chunk, chunk_sem):
    for slot in range(RING):
        pltpu.make_async_copy(lists_hbm.at[slot], chunk.at[slot], chunk_sem.at[slot]).start()


def parent_level(own, came, lists, translations, inverse, block, group, chunk_steps):
    parents = own.shape[1]
    columns, _, slots, _ = came.shape
    count = parents + columns * slots
    first = RING * chunk_steps * group

    def kernel(
        own_ref, came_ref, lists_hbm, operators_hbm, inverse_ref, out_ref,
        table, operators, total, result, chunk, chunk_sem, operator_sem,
    ):
        early, late = split_operator_copy(operators_hbm, operators, operator_sem, first)
        early.start()
        first_fetches(lists_hbm, chunk, chunk_sem)
        late.start()
        table[...] = jnp.zeros_like(table)
        total[...] = jnp.zeros_like(total)
        spread(table, 8, own_ref)
        for column in range(columns):
            spread(table, 8 + 4 * (parents + column * slots), came_ref.at[column])
        early.wait()

        def at_turn(turn):
            pl.when(turn == 1)(lambda: late.wait())

        translate_steps(
            lists_hbm, table, operators, total, chunk, chunk_sem, block, group, chunk_steps,
            at_turn,
        )
        check = total[...].reshape(4 * parents, 128).astype(jnp.bfloat16)
        result[...] = dot_nt(check, inverse_ref[...])
        for k in range(3):
            out_ref[k] = result[pl.ds(k, parents, stride=4), :].astype(jnp.bfloat16)

    vmem = pl.BlockSpec(memory_space=pltpu.VMEM)
    hbm = pl.BlockSpec(memory_space=pl.ANY)
    return pl.pallas_call(
        kernel,
        in_specs=[vmem, vmem, hbm, hbm, vmem],
        out_specs=vmem,
        out_shape=jax.ShapeDtypeStruct((3, parents, 128), jnp.bfloat16),
        scratch_shapes=[
            pltpu.VMEM((4 * count + 16, 128), jnp.float32),
            pltpu.VMEM(translations.shape, translations.dtype),
            pltpu.VMEM((parents // block, 4 * block, 128), jnp.float32),
            pltpu.VMEM((4 * parents, 128), jnp.float32),
            pltpu.SMEM((RING, 1, chunk_steps * block * group), jnp.int32),
            pltpu.SemaphoreType.DMA((RING,)),
            pltpu.SemaphoreType.DMA((2,)),
        ],
        compiler_params=pltpu.CompilerParams(vmem_limit_bytes=VMEM_BYTES),
        name="parent_level",
    )(own, came, lists, translations, inverse)


def leaf_level(
    own, came, direct, origin, parent_down, lists, translations, to_child, inverse,
    block, group, chunk_steps,
):
    boxes = own.shape[1]
    parents = boxes // 8
    offsets = origin.shape[1]
    slots = direct.shape[1]
    count = boxes + offsets * slots
    first = RING * chunk_steps * group // (boxes // block)

    def kernel(
        origin_ref, own_ref, parent_ref, to_child_ref, inverse_ref, lists_hbm, operators_hbm,
        came_hbm, direct_hbm, out_ref,
        table, operators, ghosts, total, result, chunk, chunk_sem, operator_sem, ghost_sem,
    ):
        def ghost_copy(source, j):
            return pltpu.make_async_copy(source, ghosts.at[j], ghost_sem.at[j])

        for j in range(offsets):
            kind, place = origin_ref[0, j], origin_ref[1, j]
            pl.when(kind == 0)(lambda: ghost_copy(came_hbm.at[place], j).start())
            pl.when(kind == 1)(lambda: ghost_copy(direct_hbm, j).start())
        first_fetches(lists_hbm, chunk, chunk_sem)
        early, late = split_operator_copy(operators_hbm, operators, operator_sem, first)
        early.start()
        late.start()
        table[0:8, :] = jnp.zeros((8, 128), jnp.float32)
        table[pl.ds(8 + 3, count, stride=4), :] = jnp.zeros((count, 128), jnp.float32)
        spread(table, 8, own_ref)
        result[pl.ds(3, boxes, stride=4), :] = jnp.zeros((boxes, 128), jnp.float32)
        for c in range(8):
            for k in range(3):
                result[pl.ds(4 * c + k, parents, stride=32), :] = dot_nt(
                    parent_ref[k], to_child_ref[c]
                )
        for b in range(boxes // block):
            total[b] = result[4 * block * b : 4 * block * (b + 1), :]
        for j in range(offsets):
            ghost_copy(direct_hbm, j).wait()
            spread(table, 8 + 4 * (boxes + j * slots), ghosts.at[j])
        early.wait()

        def at_turn(turn):
            pl.when(turn == 1)(lambda: late.wait())

        translate_steps(
            lists_hbm, table, operators, total, chunk, chunk_sem, block, group, chunk_steps,
            at_turn,
        )
        for b in range(boxes // block):
            result[4 * block * b : 4 * block * (b + 1), :] = dot_nt(
                total[b].astype(jnp.bfloat16), inverse_ref[...]
            )
        for k in range(3):
            out_ref[k] = result[pl.ds(k, boxes, stride=4), :].astype(jnp.bfloat16)

    vmem = pl.BlockSpec(memory_space=pltpu.VMEM)
    smem = pl.BlockSpec(memory_space=pltpu.SMEM)
    hbm = pl.BlockSpec(memory_space=pl.ANY)
    return pl.pallas_call(
        kernel,
        in_specs=[smem, vmem, vmem, vmem, vmem, hbm, hbm, hbm, hbm],
        out_specs=vmem,
        out_shape=jax.ShapeDtypeStruct((3, boxes, 128), jnp.bfloat16),
        scratch_shapes=[
            pltpu.VMEM((4 * count + 16, 128), jnp.float32),
            pltpu.VMEM(translations.shape, translations.dtype),
            pltpu.VMEM((offsets, 3, slots, 128), jnp.bfloat16),
            pltpu.VMEM((boxes // block, 4 * block, 128), jnp.float32),
            pltpu.VMEM((4 * boxes, 128), jnp.float32),
            pltpu.SMEM((RING, 1, chunk_steps * block * group), jnp.int32),
            pltpu.SemaphoreType.DMA((RING,)),
            pltpu.SemaphoreType.DMA((2,)),
            pltpu.SemaphoreType.DMA((offsets,)),
        ],
        compiler_params=pltpu.CompilerParams(vmem_limit_bytes=VMEM_BYTES),
        name="leaf_level",
    )(
        origin, own, parent_down, to_child, inverse, lists, translations, came, direct
    )


def offset_index(distance):
    return jnp.where(distance > 0, distance - 1, NEAR - 1 - distance)


def message_order(column, columns, start):
    difference = jnp.arange(columns) - column
    order = jnp.where(jnp.abs(difference) > NEAR, 0, offset_index(difference))
    beside = start + jnp.arange(NEAR - 1) - column
    beside = jnp.where(column < NEAR, beside - columns, beside + columns)
    beside = jnp.where(jnp.abs(beside) < NEAR, offset_index(beside), 0)
    last = offset_index(jnp.where(column < NEAR, -NEAR, NEAR))
    return jnp.concatenate([jnp.where(difference == 0, 0, order), beside, last[None]])


def message_origin(column, columns):
    offset = jnp.arange(2 * NEAR)
    distance = jnp.where(offset < NEAR, offset + 1, NEAR - 1 - offset)
    sender = column - distance
    inside = (sender >= 0) & (sender < columns)
    kind = jnp.where(inside | (jnp.abs(distance) < NEAR), 0, 1)
    return jnp.stack([kind, sender % columns]).astype(jnp.int32)


def local(
    leaf_up,
    child_to_parent,
    translations,
    parent_to_child,
    check_to_density,
    leaf_lists,
    leaf_ghosts,
    parent_lists,
    parent_ghosts,
):
    rows, columns = lax.axis_size("row"), lax.axis_size("col")
    column = lax.axis_index("col")
    planes = leaf_up.transpose(1, 0, 2)
    start = jnp.where(column < NEAR, NEAR + 1, 0)
    chosen = leaf_ghosts[0][message_order(column, columns, start)]
    sent, passing, direct, parent_up, parent_sent = prepare(
        planes, chosen, parent_ghosts[0], child_to_parent
    )
    parent_came = lax.all_to_all(parent_sent, "col", split_axis=0, concat_axis=0, tiled=True)
    ranks = range(rows * columns)
    turn = [(d, d - columns if d % columns < NEAR else d + columns) for d in ranks]
    shifted = lax.ppermute(passing, ("row", "col"), [p for p in turn if p[1] in ranks])
    half = [(d, d + NEAR if d % columns >= NEAR else d - NEAR) for d in ranks]
    direct = lax.ppermute(direct, ("row", "col"), [p for p in half if p[1] in ranks])
    foreign = jnp.abs(start + jnp.arange(NEAR - 1) - column) > NEAR
    kept = lax.dynamic_slice_in_dim(sent, start, NEAR - 1)
    shifted = jnp.where(foreign[:, None, None, None], shifted, kept)
    sent = lax.dynamic_update_slice_in_dim(sent, shifted, start, 0)
    sent, direct, parent_came = lax.optimization_barrier((sent, direct, parent_came))
    came = lax.all_to_all(sent, "col", split_axis=0, concat_axis=0, tiled=True)
    parent_down = parent_level(
        parent_up,
        parent_came,
        order_lists(parent_lists, 64, 4, 8),
        translations,
        check_to_density,
        64,
        4,
        8,
    )
    lists = order_lists(leaf_lists, 256, 4, 4)
    came, parent_down, lists = lax.optimization_barrier((came, parent_down, lists))
    leaf_down = leaf_level(
        planes,
        came,
        direct,
        message_origin(column, columns),
        parent_down,
        lists,
        translations,
        parent_to_child,
        check_to_density,
        256,
        4,
        4,
    )
    return leaf_down.transpose(1, 0, 2)


def solution(mesh):
    return jax.shard_map(
        local,
        mesh=mesh,
        in_specs=(
            P(("row", "col"), None, None),
            P(),
            P(),
            P(),
            P(),
            P(("row", "col"), None),
            P(("row", "col"), None, None),
            P(("row", "col"), None),
            P(("row", "col"), None, None),
        ),
        out_specs=P(("row", "col"), None, None),
        check_vma=False,
    )
```

```python
import jax
import jax.numpy as jnp
from jax import lax
from jax.experimental import pallas as pl
from jax.experimental.pallas import tpu as pltpu
from jax.sharding import PartitionSpec as P

RING = 2
NEAR = 8
VMEM_BYTES = 58 * 2**20


def dot_nt(left, right):
    return lax.dot_general(
        left, right, (((1,), (1,)), ((), ())), preferred_element_type=jnp.float32
    )


def pick_pair(table, low_half, first, second):
    upper = table[pl.ds(first + 4, 8), :]
    lower = table[pl.ds(second, 8), :]
    return jnp.where(low_half, upper, lower)


def spread(table, at, planes_ref):
    for k in range(3):
        plane = planes_ref[k]
        table[pl.ds(at + k, plane.shape[0], stride=4), :] = plane.astype(jnp.float32)


def select_rows(table, places_ref, start, count, scale, gathered, out_ref):
    low_half = lax.broadcasted_iota(jnp.int32, (8, 128), 0) < 4
    for pair in range(count // 2):
        at = start + 2 * pair
        gathered[8 * pair : 8 * pair + 8, :] = pick_pair(
            table, low_half, scale * places_ref[0, at], scale * places_ref[0, at + 1]
        )
    for k in range(3):
        out_ref[k] = gathered[pl.ds(k, count, stride=4), :].astype(jnp.bfloat16)


def prepare(planes, ghosts, parent_ghosts, operators):
    boxes = planes.shape[1]
    parents = boxes // 8
    messages, slots = ghosts.shape
    columns, parent_slots = parent_ghosts.shape
    passed = messages - columns - 1

    def kernel(
        planes_ref, ghosts_ref, parent_ghosts_ref, operators_ref,
        sent_ref, passing_ref, direct_ref, up_ref, parent_sent_ref,
        table, own, gathered, parent_gathered,
    ):
        spread(table, 4, planes_ref)
        matrices = jnp.concatenate([operators_ref[c] for c in range(8)], axis=1)
        for k in range(3):
            children = jnp.concatenate(
                [table[pl.ds(4 + 4 * c + k, parents, stride=32), :] for c in range(8)], axis=1
            )
            up_ref[k] = dot_nt(children.astype(jnp.bfloat16), matrices).astype(jnp.bfloat16)
        spread(own, 4, up_ref)
        for column in range(columns):
            select_rows(
                own, parent_ghosts_ref, column * parent_slots, parent_slots, 4, parent_gathered,
                parent_sent_ref.at[column],
            )
        targets = [sent_ref.at[i] for i in range(columns)]
        targets += [passing_ref.at[i] for i in range(passed)] + [direct_ref]
        for which, target in enumerate(targets):
            select_rows(table, ghosts_ref, which * slots, slots, 1, gathered, target)

    vmem = pl.BlockSpec(memory_space=pltpu.VMEM)
    smem = pl.BlockSpec(memory_space=pltpu.SMEM)
    return pl.pallas_call(
        kernel,
        in_specs=[vmem, smem, smem, vmem],
        out_specs=[vmem] * 5,
        out_shape=[
            jax.ShapeDtypeStruct((columns, 3, slots, 128), jnp.bfloat16),
            jax.ShapeDtypeStruct((passed, 3, slots, 128), jnp.bfloat16),
            jax.ShapeDtypeStruct((3, slots, 128), jnp.bfloat16),
            jax.ShapeDtypeStruct((3, parents, 128), jnp.bfloat16),
            jax.ShapeDtypeStruct((columns, 3, parent_slots, 128), jnp.bfloat16),
        ],
        scratch_shapes=[
            pltpu.VMEM((4 * boxes + 16, 128), jnp.float32),
            pltpu.VMEM((4 * parents + 16, 128), jnp.float32),
            pltpu.VMEM((4 * slots, 128), jnp.float32),
            pltpu.VMEM((4 * parent_slots, 128), jnp.float32),
        ],
        compiler_params=pltpu.CompilerParams(vmem_limit_bytes=VMEM_BYTES),
        name="prepare",
    )(
        planes, (ghosts * 4).reshape(1, -1), parent_ghosts.reshape(1, -1), operators
    )


def order_lists(lists, block, group, chunk_steps):
    boxes, vectors = lists.shape
    places = (lists + 1) * 4
    places = places.T.reshape(vectors // group, group, boxes // block, block)
    places = places.transpose(0, 2, 1, 3).reshape(-1, group * block)
    padding = -places.shape[0] % (RING * chunk_steps) + RING * chunk_steps
    places = jnp.concatenate(
        [places, jnp.zeros((padding, group * block), places.dtype)], axis=0
    )
    return places.reshape(-1, 1, chunk_steps * group * block)


def translate_steps(
    lists_hbm, table, operators, total, chunk, chunk_sem, block, group, chunk_steps, at_turn
):
    blocks = total.shape[0]
    groups = operators.shape[0] // group
    chunks = lists_hbm.shape[0] - RING
    size = block * group
    low_half = lax.broadcasted_iota(jnp.int32, (8, 128), 0) < 4

    def fetch(at, slot):
        return pltpu.make_async_copy(lists_hbm.at[at], chunk.at[slot], chunk_sem.at[slot])

    def round_of_chunks(turn, _):
        at_turn(turn)
        for slot in range(RING):
            fetch(turn * RING + slot, slot).wait()
            for h in range(chunk_steps):
                which = ((turn * RING + slot) * chunk_steps + h) // blocks
                which = jnp.minimum(which, groups - 1)
                columns = []
                for t in range(group):
                    rows = []
                    for pair in range(block // 2):
                        at = h * size + t * block + 2 * pair
                        rows.append(
                            pick_pair(table, low_half, chunk[slot, 0, at], chunk[slot, 0, at + 1])
                        )
                    columns.append(jnp.concatenate(rows, axis=0).astype(jnp.bfloat16))
                sources = jnp.concatenate(columns, axis=1)
                matrices = jnp.concatenate(
                    [operators[which * group + t] for t in range(group)], axis=1
                )
                total[h % blocks] += dot_nt(sources, matrices)
            fetch((turn + 1) * RING + slot, slot).start()
        return 0

    lax.fori_loop(0, chunks // RING, round_of_chunks, 0)
    for slot in range(RING):
        fetch(chunks + slot, slot).wait()


def split_operator_copy(operators_hbm, operators, sems, first):
    return (
        pltpu.make_async_copy(
            operators_hbm.at[pl.ds(0, first)], operators.at[pl.ds(0, first)], sems.at[0]
        ),
        pltpu.make_async_copy(
            operators_hbm.at[pl.ds(first, operators.shape[0] - first)],
            operators.at[pl.ds(first, operators.shape[0] - first)],
            sems.at[1],
        ),
    )


def first_fetches(lists_hbm, chunk, chunk_sem):
    for slot in range(RING):
        pltpu.make_async_copy(lists_hbm.at[slot], chunk.at[slot], chunk_sem.at[slot]).start()


def parent_level(
    own, came, lists, translations, inverse, to_child, block, group, chunk_steps
):
    parents = own.shape[1]
    columns, _, slots, _ = came.shape
    count = parents + columns * slots
    first = RING * chunk_steps * group

    def kernel(
        own_ref, came_ref, lists_hbm, operators_hbm, inverse_ref, to_child_ref, out_ref,
        table, operators, total, result, chunk, chunk_sem, operator_sem,
    ):
        early, late = split_operator_copy(operators_hbm, operators, operator_sem, first)
        early.start()
        first_fetches(lists_hbm, chunk, chunk_sem)
        late.start()
        table[...] = jnp.zeros_like(table)
        total[...] = jnp.zeros_like(total)
        spread(table, 8, own_ref)
        for column in range(columns):
            spread(table, 8 + 4 * (parents + column * slots), came_ref.at[column])
        early.wait()

        def at_turn(turn):
            pl.when(turn == 1)(lambda: late.wait())

        translate_steps(
            lists_hbm, table, operators, total, chunk, chunk_sem, block, group, chunk_steps,
            at_turn,
        )
        check = total[...].reshape(4 * parents, 128).astype(jnp.bfloat16)
        result[...] = dot_nt(check, inverse_ref[...])
        out_ref[pl.ds(3, 8 * parents, stride=4), :] = jnp.zeros((8 * parents, 128), jnp.float32)
        for k in range(3):
            down = result[pl.ds(k, parents, stride=4), :].astype(jnp.bfloat16)
            for c in range(8):
                out_ref[pl.ds(4 * c + k, parents, stride=32), :] = dot_nt(down, to_child_ref[c])

    vmem = pl.BlockSpec(memory_space=pltpu.VMEM)
    hbm = pl.BlockSpec(memory_space=pl.ANY)
    return pl.pallas_call(
        kernel,
        in_specs=[vmem, vmem, hbm, hbm, vmem, vmem],
        out_specs=vmem,
        out_shape=jax.ShapeDtypeStruct((32 * parents, 128), jnp.float32),
        scratch_shapes=[
            pltpu.VMEM((4 * count + 16, 128), jnp.float32),
            pltpu.VMEM(translations.shape, translations.dtype),
            pltpu.VMEM((parents // block, 4 * block, 128), jnp.float32),
            pltpu.VMEM((4 * parents, 128), jnp.float32),
            pltpu.SMEM((RING, 1, chunk_steps * block * group), jnp.int32),
            pltpu.SemaphoreType.DMA((RING,)),
            pltpu.SemaphoreType.DMA((2,)),
        ],
        compiler_params=pltpu.CompilerParams(vmem_limit_bytes=VMEM_BYTES),
        name="parent_level",
    )(own, came, lists, translations, inverse, to_child)


def leaf_level(
    own, came, direct, origin, from_parent, lists, translations, inverse, block, group, chunk_steps,
):
    boxes = own.shape[1]
    offsets = origin.shape[1]
    slots = direct.shape[1]
    count = boxes + offsets * slots
    first = RING * chunk_steps * group // (boxes // block)

    def kernel(
        origin_ref, own_ref, parent_hbm, inverse_ref, lists_hbm, operators_hbm, came_ref,
        direct_ref, out_ref,
        table, operators, total, result, chunk, chunk_sem, operator_sem, parent_sem,
    ):
        first_fetches(lists_hbm, chunk, chunk_sem)
        early, late = split_operator_copy(operators_hbm, operators, operator_sem, first)
        early.start()
        parent_copy = pltpu.make_async_copy(parent_hbm, total, parent_sem)
        parent_copy.start()
        late.start()
        table[0:8, :] = jnp.zeros((8, 128), jnp.float32)
        table[pl.ds(8 + 3, count, stride=4), :] = jnp.zeros((count, 128), jnp.float32)
        spread(table, 8, own_ref)
        for j in range(offsets):
            at = 8 + 4 * (boxes + j * slots)
            spread(table, at, came_ref.at[origin_ref[1, j]])
            if j % NEAR == NEAR - 1:
                pl.when(origin_ref[0, j] == 1)(lambda: spread(table, at, direct_ref))
        early.wait()
        parent_copy.wait()

        def at_turn(turn):
            pl.when(turn == 1)(lambda: late.wait())

        translate_steps(
            lists_hbm, table, operators, total, chunk, chunk_sem, block, group, chunk_steps,
            at_turn,
        )
        for b in range(boxes // block):
            result[4 * block * b : 4 * block * (b + 1), :] = dot_nt(
                total[b].astype(jnp.bfloat16), inverse_ref[...]
            )
        for k in range(3):
            out_ref[k] = result[pl.ds(k, boxes, stride=4), :].astype(jnp.bfloat16)

    vmem = pl.BlockSpec(memory_space=pltpu.VMEM)
    smem = pl.BlockSpec(memory_space=pltpu.SMEM)
    hbm = pl.BlockSpec(memory_space=pl.ANY)
    return pl.pallas_call(
        kernel,
        in_specs=[smem, vmem, hbm, vmem, hbm, hbm, vmem, vmem],
        out_specs=vmem,
        out_shape=jax.ShapeDtypeStruct((3, boxes, 128), jnp.bfloat16),
        scratch_shapes=[
            pltpu.VMEM((4 * count + 16, 128), jnp.float32),
            pltpu.VMEM(translations.shape, translations.dtype),
            pltpu.VMEM((boxes // block, 4 * block, 128), jnp.float32),
            pltpu.VMEM((4 * boxes, 128), jnp.float32),
            pltpu.SMEM((RING, 1, chunk_steps * block * group), jnp.int32),
            pltpu.SemaphoreType.DMA((RING,)),
            pltpu.SemaphoreType.DMA((2,)),
            pltpu.SemaphoreType.DMA,
        ],
        compiler_params=pltpu.CompilerParams(vmem_limit_bytes=VMEM_BYTES),
        name="leaf_level",
    )(
        origin,
        own,
        from_parent.reshape(boxes // block, 4 * block, 128),
        inverse,
        lists,
        translations,
        came,
        direct,
    )


def offset_index(distance):
    return jnp.where(distance > 0, distance - 1, NEAR - 1 - distance)


def message_order(column, columns, start):
    difference = jnp.arange(columns) - column
    order = jnp.where(jnp.abs(difference) > NEAR, 0, offset_index(difference))
    beside = start + jnp.arange(NEAR - 1) - column
    beside = jnp.where(column < NEAR, beside - columns, beside + columns)
    beside = jnp.where(jnp.abs(beside) < NEAR, offset_index(beside), 0)
    last = offset_index(jnp.where(column < NEAR, -NEAR, NEAR))
    return jnp.concatenate([jnp.where(difference == 0, 0, order), beside, last[None]])


def message_origin(column, columns):
    offset = jnp.arange(2 * NEAR)
    distance = jnp.where(offset < NEAR, offset + 1, NEAR - 1 - offset)
    sender = column - distance
    inside = (sender >= 0) & (sender < columns)
    kind = jnp.where(inside | (jnp.abs(distance) < NEAR), 0, 1)
    return jnp.stack([kind, sender % columns]).astype(jnp.int32)


def local(
    leaf_up,
    child_to_parent,
    translations,
    parent_to_child,
    check_to_density,
    leaf_lists,
    leaf_ghosts,
    parent_lists,
    parent_ghosts,
):
    rows, columns = lax.axis_size("row"), lax.axis_size("col")
    column = lax.axis_index("col")
    planes = leaf_up.transpose(1, 0, 2)
    start = jnp.where(column < NEAR, NEAR + 1, 0)
    chosen = leaf_ghosts[0][message_order(column, columns, start)]
    sent, passing, direct, parent_up, parent_sent = prepare(
        planes, chosen, parent_ghosts[0], child_to_parent
    )
    parent_came = lax.all_to_all(parent_sent, "col", split_axis=0, concat_axis=0, tiled=True)
    ranks = range(rows * columns)
    turn = [(d, d - columns if d % columns < NEAR else d + columns) for d in ranks]
    shifted = lax.ppermute(passing, ("row", "col"), [p for p in turn if p[1] in ranks])
    half = [(d, d + NEAR if d % columns >= NEAR else d - NEAR) for d in ranks]
    direct = lax.ppermute(direct, ("row", "col"), [p for p in half if p[1] in ranks])
    foreign = jnp.abs(start + jnp.arange(NEAR - 1) - column) > NEAR
    kept = lax.dynamic_slice_in_dim(sent, start, NEAR - 1)
    shifted = jnp.where(foreign[:, None, None, None], shifted, kept)
    sent = lax.dynamic_update_slice_in_dim(sent, shifted, start, 0)
    sent, parent_came = lax.optimization_barrier((sent, parent_came))
    came = lax.all_to_all(sent, "col", split_axis=0, concat_axis=0, tiled=True)
    from_parent = parent_level(
        parent_up,
        parent_came,
        order_lists(parent_lists, 64, 4, 8),
        translations,
        check_to_density,
        parent_to_child,
        64,
        4,
        8,
    )
    lists = order_lists(leaf_lists, 256, 4, 4)
    came, from_parent, lists = lax.optimization_barrier((came, from_parent, lists))
    leaf_down = leaf_level(
        planes,
        came,
        direct,
        message_origin(column, columns),
        from_parent,
        lists,
        translations,
        check_to_density,
        256,
        4,
        4,
    )
    return leaf_down.transpose(1, 0, 2)


def solution(mesh):
    return jax.shard_map(
        local,
        mesh=mesh,
        in_specs=(
            P(("row", "col"), None, None),
            P(),
            P(),
            P(),
            P(),
            P(("row", "col"), None),
            P(("row", "col"), None, None),
            P(("row", "col"), None),
            P(("row", "col"), None, None),
        ),
        out_specs=P(("row", "col"), None, None),
        check_vma=False,
    )
```

```python
import jax
import jax.numpy as jnp
from jax import lax
from jax.experimental import pallas as pl
from jax.experimental.pallas import tpu as pltpu
from jax.sharding import PartitionSpec as P

RING = 2
NEAR = 8
VMEM_BYTES = 58 * 2**20


def dot_nt(left, right):
    return lax.dot_general(
        left, right, (((1,), (1,)), ((), ())), preferred_element_type=jnp.float32
    )


def pick_pair(table, low_half, first, second):
    upper = table[pl.ds(first + 4, 8), :]
    lower = table[pl.ds(second, 8), :]
    return jnp.where(low_half, upper, lower)


def spread(table, at, planes_ref):
    for k in range(3):
        plane = planes_ref[k]
        table[pl.ds(at + k, plane.shape[0], stride=4), :] = plane.astype(jnp.float32)


def select_rows(table, places_ref, start, count, scale, gathered, out_ref):
    low_half = lax.broadcasted_iota(jnp.int32, (8, 128), 0) < 4
    for pair in range(count // 2):
        at = start + 2 * pair
        gathered[8 * pair : 8 * pair + 8, :] = pick_pair(
            table, low_half, scale * places_ref[0, at], scale * places_ref[0, at + 1]
        )
    for k in range(3):
        out_ref[k] = gathered[pl.ds(k, count, stride=4), :].astype(jnp.bfloat16)


def prepare(planes, ghosts, parent_ghosts, operators):
    boxes = planes.shape[1]
    parents = boxes // 8
    messages, slots = ghosts.shape
    columns, parent_slots = parent_ghosts.shape
    passed = messages - columns - 1

    def kernel(
        planes_ref, ghosts_ref, parent_ghosts_ref, operators_ref,
        sent_ref, passing_ref, direct_ref, up_ref, parent_sent_ref,
        table, own, gathered, parent_gathered,
    ):
        spread(table, 4, planes_ref)
        matrices = jnp.concatenate([operators_ref[c] for c in range(8)], axis=1)
        for k in range(3):
            children = jnp.concatenate(
                [table[pl.ds(4 + 4 * c + k, parents, stride=32), :] for c in range(8)], axis=1
            )
            up_ref[k] = dot_nt(children.astype(jnp.bfloat16), matrices).astype(jnp.bfloat16)
        spread(own, 4, up_ref)
        for column in range(columns):
            select_rows(
                own, parent_ghosts_ref, column * parent_slots, parent_slots, 4, parent_gathered,
                parent_sent_ref.at[column],
            )
        targets = [sent_ref.at[i] for i in range(columns)]
        targets += [passing_ref.at[i] for i in range(passed)] + [direct_ref]
        for which, target in enumerate(targets):
            select_rows(table, ghosts_ref, which * slots, slots, 1, gathered, target)

    vmem = pl.BlockSpec(memory_space=pltpu.VMEM)
    smem = pl.BlockSpec(memory_space=pltpu.SMEM)
    return pl.pallas_call(
        kernel,
        in_specs=[vmem, smem, smem, vmem],
        out_specs=[vmem] * 5,
        out_shape=[
            jax.ShapeDtypeStruct((columns, 3, slots, 128), jnp.bfloat16),
            jax.ShapeDtypeStruct((passed, 3, slots, 128), jnp.bfloat16),
            jax.ShapeDtypeStruct((3, slots, 128), jnp.bfloat16),
            jax.ShapeDtypeStruct((3, parents, 128), jnp.bfloat16),
            jax.ShapeDtypeStruct((columns, 3, parent_slots, 128), jnp.bfloat16),
        ],
        scratch_shapes=[
            pltpu.VMEM((4 * boxes + 16, 128), jnp.float32),
            pltpu.VMEM((4 * parents + 16, 128), jnp.float32),
            pltpu.VMEM((4 * slots, 128), jnp.float32),
            pltpu.VMEM((4 * parent_slots, 128), jnp.float32),
        ],
        compiler_params=pltpu.CompilerParams(vmem_limit_bytes=VMEM_BYTES),
        name="prepare",
    )(
        planes, (ghosts * 4).reshape(1, -1), parent_ghosts.reshape(1, -1), operators
    )


def order_lists(lists, block, group, chunk_steps):
    boxes, vectors = lists.shape
    places = (lists + 1) * 4
    places = places.T.reshape(vectors // group, group, boxes // block, block)
    places = places.transpose(0, 2, 1, 3).reshape(-1, group * block)
    padding = -places.shape[0] % (RING * chunk_steps) + RING * chunk_steps
    places = jnp.concatenate(
        [places, jnp.zeros((padding, group * block), places.dtype)], axis=0
    )
    return places.reshape(-1, 1, chunk_steps * group * block)


def translate_steps(
    lists_hbm, table, operators, total, chunk, chunk_sem, block, group, chunk_steps, at_turn
):
    blocks = total.shape[0]
    groups = operators.shape[0] // group
    chunks = lists_hbm.shape[0] - RING
    size = block * group
    low_half = lax.broadcasted_iota(jnp.int32, (8, 128), 0) < 4

    def fetch(at, slot):
        return pltpu.make_async_copy(lists_hbm.at[at], chunk.at[slot], chunk_sem.at[slot])

    def round_of_chunks(turn, _):
        at_turn(turn)
        for slot in range(RING):
            fetch(turn * RING + slot, slot).wait()
            for h in range(chunk_steps):
                which = ((turn * RING + slot) * chunk_steps + h) // blocks
                which = jnp.minimum(which, groups - 1)
                columns = []
                for t in range(group):
                    rows = []
                    for pair in range(block // 2):
                        at = h * size + t * block + 2 * pair
                        rows.append(
                            pick_pair(table, low_half, chunk[slot, 0, at], chunk[slot, 0, at + 1])
                        )
                    columns.append(jnp.concatenate(rows, axis=0).astype(jnp.bfloat16))
                sources = jnp.concatenate(columns, axis=1)
                matrices = jnp.concatenate(
                    [operators[which * group + t] for t in range(group)], axis=1
                )
                total[h % blocks] += dot_nt(sources, matrices)
            fetch((turn + 1) * RING + slot, slot).start()
        return 0

    lax.fori_loop(0, chunks // RING, round_of_chunks, 0)
    for slot in range(RING):
        fetch(chunks + slot, slot).wait()


def split_operator_copy(operators_hbm, operators, sems, first):
    return (
        pltpu.make_async_copy(
            operators_hbm.at[pl.ds(0, first)], operators.at[pl.ds(0, first)], sems.at[0]
        ),
        pltpu.make_async_copy(
            operators_hbm.at[pl.ds(first, operators.shape[0] - first)],
            operators.at[pl.ds(first, operators.shape[0] - first)],
            sems.at[1],
        ),
    )


def first_fetches(lists_hbm, chunk, chunk_sem):
    for slot in range(RING):
        pltpu.make_async_copy(lists_hbm.at[slot], chunk.at[slot], chunk_sem.at[slot]).start()


def parent_level(
    own, came, lists, translations, inverse, to_child, block, group, chunk_steps
):
    parents = own.shape[1]
    columns, _, slots, _ = came.shape
    count = parents + columns * slots
    first = RING * chunk_steps * group

    def kernel(
        own_ref, came_ref, lists_hbm, operators_hbm, inverse_ref, to_child_ref, out_ref,
        table, operators, total, result, chunk, chunk_sem, operator_sem,
    ):
        early, late = split_operator_copy(operators_hbm, operators, operator_sem, first)
        early.start()
        first_fetches(lists_hbm, chunk, chunk_sem)
        late.start()
        table[...] = jnp.zeros_like(table)
        total[...] = jnp.zeros_like(total)
        spread(table, 8, own_ref)
        for column in range(columns):
            spread(table, 8 + 4 * (parents + column * slots), came_ref.at[column])
        early.wait()

        def at_turn(turn):
            pl.when(turn == 1)(lambda: late.wait())

        translate_steps(
            lists_hbm, table, operators, total, chunk, chunk_sem, block, group, chunk_steps,
            at_turn,
        )
        check = total[...].reshape(4 * parents, 128).astype(jnp.bfloat16)
        result[...] = dot_nt(check, inverse_ref[...])
        out_ref[pl.ds(3, 8 * parents, stride=4), :] = jnp.zeros((8 * parents, 128), jnp.float32)
        for k in range(3):
            down = result[pl.ds(k, parents, stride=4), :].astype(jnp.bfloat16)
            for c in range(8):
                out_ref[pl.ds(4 * c + k, parents, stride=32), :] = dot_nt(down, to_child_ref[c])

    vmem = pl.BlockSpec(memory_space=pltpu.VMEM)
    hbm = pl.BlockSpec(memory_space=pl.ANY)
    return pl.pallas_call(
        kernel,
        in_specs=[vmem, vmem, hbm, hbm, vmem, vmem],
        out_specs=vmem,
        out_shape=jax.ShapeDtypeStruct((32 * parents, 128), jnp.float32),
        scratch_shapes=[
            pltpu.VMEM((4 * count + 16, 128), jnp.float32),
            pltpu.VMEM(translations.shape, translations.dtype),
            pltpu.VMEM((parents // block, 4 * block, 128), jnp.float32),
            pltpu.VMEM((4 * parents, 128), jnp.float32),
            pltpu.SMEM((RING, 1, chunk_steps * block * group), jnp.int32),
            pltpu.SemaphoreType.DMA((RING,)),
            pltpu.SemaphoreType.DMA((2,)),
        ],
        compiler_params=pltpu.CompilerParams(vmem_limit_bytes=VMEM_BYTES),
        name="parent_level",
    )(own, came, lists, translations, inverse, to_child)


def leaf_level(
    own, came, direct, origin, from_parent, lists, translations, inverse, block, group, chunk_steps,
):
    boxes = own.shape[1]
    offsets = origin.shape[1]
    slots = direct.shape[1]
    count = boxes + offsets * slots
    first = RING * chunk_steps * group // (boxes // block)

    def kernel(
        origin_ref, own_ref, parent_hbm, inverse_ref, lists_hbm, operators_hbm, came_ref,
        direct_ref, out_ref,
        table, operators, total, result, chunk, chunk_sem, operator_sem, parent_sem,
    ):
        first_fetches(lists_hbm, chunk, chunk_sem)
        early, late = split_operator_copy(operators_hbm, operators, operator_sem, first)
        early.start()
        parent_copy = pltpu.make_async_copy(parent_hbm, total, parent_sem)
        parent_copy.start()
        late.start()
        table[0:8, :] = jnp.zeros((8, 128), jnp.float32)
        table[pl.ds(8 + 3, count, stride=4), :] = jnp.zeros((count, 128), jnp.float32)
        spread(table, 8, own_ref)
        for j in range(offsets):
            at = 8 + 4 * (boxes + j * slots)
            spread(table, at, came_ref.at[origin_ref[1, j]])
            if j % NEAR == NEAR - 1:
                pl.when(origin_ref[0, j] == 1)(lambda: spread(table, at, direct_ref))
        early.wait()
        parent_copy.wait()

        def at_turn(turn):
            pl.when(turn == 1)(lambda: late.wait())

        translate_steps(
            lists_hbm, table, operators, total, chunk, chunk_sem, block, group, chunk_steps,
            at_turn,
        )
        for b in range(boxes // block):
            result[4 * block * b : 4 * block * (b + 1), :] = dot_nt(
                total[b].astype(jnp.bfloat16), inverse_ref[...]
            )
        for k in range(3):
            out_ref[k] = result[pl.ds(k, boxes, stride=4), :].astype(jnp.bfloat16)

    vmem = pl.BlockSpec(memory_space=pltpu.VMEM)
    smem = pl.BlockSpec(memory_space=pltpu.SMEM)
    hbm = pl.BlockSpec(memory_space=pl.ANY)
    return pl.pallas_call(
        kernel,
        in_specs=[smem, vmem, hbm, vmem, hbm, hbm, vmem, vmem],
        out_specs=vmem,
        out_shape=jax.ShapeDtypeStruct((3, boxes, 128), jnp.bfloat16),
        scratch_shapes=[
            pltpu.VMEM((4 * count + 16, 128), jnp.float32),
            pltpu.VMEM(translations.shape, translations.dtype),
            pltpu.VMEM((boxes // block, 4 * block, 128), jnp.float32),
            pltpu.VMEM((4 * boxes, 128), jnp.float32),
            pltpu.SMEM((RING, 1, chunk_steps * block * group), jnp.int32),
            pltpu.SemaphoreType.DMA((RING,)),
            pltpu.SemaphoreType.DMA((2,)),
            pltpu.SemaphoreType.DMA,
        ],
        compiler_params=pltpu.CompilerParams(vmem_limit_bytes=VMEM_BYTES),
        name="leaf_level",
    )(
        origin,
        own,
        from_parent.reshape(boxes // block, 4 * block, 128),
        inverse,
        lists,
        translations,
        came,
        direct,
    )


def offset_index(distance):
    return jnp.where(distance > 0, distance - 1, NEAR - 1 - distance)


def message_order(column, columns, start):
    difference = jnp.arange(columns) - column
    order = jnp.where(jnp.abs(difference) > NEAR, 0, offset_index(difference))
    beside = start + jnp.arange(NEAR - 1) - column
    beside = jnp.where(column < NEAR, beside - columns, beside + columns)
    beside = jnp.where(jnp.abs(beside) < NEAR, offset_index(beside), 0)
    last = offset_index(jnp.where(column < NEAR, -NEAR, NEAR))
    return jnp.concatenate([jnp.where(difference == 0, 0, order), beside, last[None]])


def message_origin(column, columns):
    offset = jnp.arange(2 * NEAR)
    distance = jnp.where(offset < NEAR, offset + 1, NEAR - 1 - offset)
    sender = column - distance
    inside = (sender >= 0) & (sender < columns)
    kind = jnp.where(inside | (jnp.abs(distance) < NEAR), 0, 1)
    return jnp.stack([kind, sender % columns]).astype(jnp.int32)


def local(
    leaf_up,
    child_to_parent,
    translations,
    parent_to_child,
    check_to_density,
    leaf_lists,
    leaf_ghosts,
    parent_lists,
    parent_ghosts,
):
    rows, columns = lax.axis_size("row"), lax.axis_size("col")
    column = lax.axis_index("col")
    planes = leaf_up.transpose(1, 0, 2)
    start = jnp.where(column < NEAR, NEAR + 1, 0)
    chosen = leaf_ghosts[0][message_order(column, columns, start)]
    sent, passing, direct, parent_up, parent_sent = prepare(
        planes, chosen, parent_ghosts[0], child_to_parent
    )
    parent_came = lax.all_to_all(parent_sent, "col", split_axis=0, concat_axis=0, tiled=True)
    ranks = range(rows * columns)
    turn = [(d, d - columns if d % columns < NEAR else d + columns) for d in ranks]
    shifted = lax.ppermute(passing, ("row", "col"), [p for p in turn if p[1] in ranks])
    half = [(d, d + NEAR if d % columns >= NEAR else d - NEAR) for d in ranks]
    direct = lax.ppermute(direct, ("row", "col"), [p for p in half if p[1] in ranks])
    foreign = jnp.abs(start + jnp.arange(NEAR - 1) - column) > NEAR
    kept = lax.dynamic_slice_in_dim(sent, start, NEAR - 1)
    shifted = jnp.where(foreign[:, None, None, None], shifted, kept)
    sent = lax.dynamic_update_slice_in_dim(sent, shifted, start, 0)
    sent, direct, parent_came = lax.optimization_barrier((sent, direct, parent_came))
    came = lax.all_to_all(sent, "col", split_axis=0, concat_axis=0, tiled=True)
    from_parent = parent_level(
        parent_up,
        parent_came,
        order_lists(parent_lists, 64, 4, 8),
        translations,
        check_to_density,
        parent_to_child,
        64,
        4,
        8,
    )
    lists = order_lists(leaf_lists, 256, 4, 4)
    came, from_parent, lists = lax.optimization_barrier((came, from_parent, lists))
    leaf_down = leaf_level(
        planes,
        came,
        direct,
        message_origin(column, columns),
        from_parent,
        lists,
        translations,
        check_to_density,
        256,
        4,
        4,
    )
    return leaf_down.transpose(1, 0, 2)


def solution(mesh):
    return jax.shard_map(
        local,
        mesh=mesh,
        in_specs=(
            P(("row", "col"), None, None),
            P(),
            P(),
            P(),
            P(),
            P(("row", "col"), None),
            P(("row", "col"), None, None),
            P(("row", "col"), None),
            P(("row", "col"), None, None),
        ),
        out_specs=P(("row", "col"), None, None),
        check_vma=False,
    )
```
